32 devices in a mesh: comp: 4 (over z), tile: 8 (over y, x, core).
Axes of the slice: x: 2, y: 2, z: 4, core: 2. Of those that a mesh axis runs over, the one named last changes fastest.
Arguments:
- vertical_profile_fields: float32 [192, 65536], P(None, ('comp', 'tile')), may hold values from -6 to 6
- implicit_diffusion_solver: float32 [192, 192], replicated, may hold values from -0.4375 to 0.4375
- prior_seawater_warmth: float32 [65536], P(('comp', 'tile')), may hold values from -6 to 6
- overlay_share_matrices: float32 [32, 256, 512], P('comp'), may hold values from 0.0009765625 to 0.015625
- overlay_pairings: int32 [3, 2048], P(None, ('comp', 'tile')), may hold values from 0 to 255, as said below
- marine_top_fields: float32 [4, 128, 4096], P(None, 'comp', 'tile'), may hold values from -6 to 6
- marine_indicator: int32 [128, 4096], P('comp', 'tile'), may hold values 0 or 1
Outputs:
- atm_new: float32 [192, 65536], P(None, ('comp', 'tile'))
- marine_fields_stepped: float32 [4, 128, 4096], P(None, 'comp', 'tile')
- seawater_warmth_regridded: float32 [65536], P(('comp', 'tile'))
The draws below stay inside these ranges and needn't reach their ends.
Inputs may be any that keep to these rules, and one draw needn't show every extreme that they name: `overlay_pairings`: row 0: on the device at comp c, tile t each id is j * 8 + t with j < 8, and each of its 8 blocks is named at least once. Row 1: ids of ocean blocks of the same band, q * 32 + r for row r of the ocean tile of tile index q; each device names every ocean tile either 0 or exactly 16 times, and in every band one ocean tile is named 16 times by every device of the band. Row 2: weight block indices below 8.
All inputs are finite; a program needn't handle non-finite values. No bound on the sum of `marine_indicator` on one device may be relied on, other than what follows from the above.
Results may differ from the reference program's by a relative error of at most 0.0003.
Values sent between devices are 32-bit elements; how exact they have to be, the bound alone decides.
A program may use at most 64 MiB of HBM per device.

```python
import math
import jax
import jax.numpy as jnp
from jax import lax

VERTICAL_LAYERS = 48
VL = 192
F = 4
BA = 256
BO = 512
ABLK = 8
OVL_DEV = 64
WTAB = 8
OX = 32
SUB = 20
TOTAL_VERTICALS = 65536
NOX = 128
NOY = 4096
N_COMP = 4
N_TILE = 8


def draw_overlay_pairings(key, part):
    key = jax.random.fold_in(key, 7)
    key_busy, key_pick, key_slot, key_row, key_table, key_block, key_order = jax.random.split(key, 7)
    capacity = max(2, 2 * OVL_DEV // N_TILE)
    partners = OVL_DEV // capacity
    devices = N_COMP * N_TILE
    busiest = jax.random.randint(key_busy, (N_COMP,), 0, N_TILE)
    pick_keys = jax.random.split(key_pick, devices)
    remaining = jax.vmap(lambda subkey: jax.random.permutation(subkey, N_TILE - 1))(pick_keys)
    busiest_dev = jnp.repeat(busiest, N_TILE)
    chosen = (busiest_dev[:, None] + 1 + remaining[:, :partners - 1]) % N_TILE
    targets = jnp.concatenate([busiest_dev[:, None], chosen], axis=1)
    targets = jnp.repeat(targets, capacity, axis=1)
    slot_keys = jax.random.split(key_slot, devices)
    targets = jax.vmap(lambda subkey, values: jax.random.permutation(subkey, values))(slot_keys, targets)
    ocean_rows = jax.random.randint(key_row, (devices, OVL_DEV), 0, OX)
    tables = jax.random.randint(key_table, (devices, OVL_DEV), 0, WTAB)
    spare_blocks = jax.random.randint(key_block, (devices, OVL_DEV), 0, ABLK)
    positions = jnp.arange(OVL_DEV)
    blocks = jnp.where(positions[None, :] < ABLK, positions[None, :], spare_blocks)
    order_keys = jax.random.split(key_order, devices)
    blocks = jax.vmap(lambda subkey, values: jax.random.permutation(subkey, values))(order_keys, blocks)
    tile_of = jnp.arange(devices) % N_TILE
    air_ids = blocks * N_TILE + tile_of[:, None]
    ocean_ids = targets * OX + ocean_rows
    return jnp.stack([air_ids.reshape(-1), ocean_ids.reshape(-1), tables.reshape(-1)]).astype(jnp.int32)


def plant(drawn, rng, smallest, largest):
    longest = drawn.shape.index(max(drawn.shape))
    spots = []
    for shift in (0, 1):
        where = [jax.random.randint(jax.random.fold_in(rng, axis), (), 0, length) for axis, length in enumerate(drawn.shape)]
        where[longest] = (where[longest] + shift) % drawn.shape[longest]
        spots.append(tuple(where))
    return drawn.at[spots[0]].set(smallest).at[spots[1]].set(largest)


def shard_levels(own_key, dims, shards, low, high):
    factor_of = 1.0
    for position, parts in shards:
        steps = jax.random.uniform(jax.random.fold_in(jax.random.fold_in(own_key, 6), position), (parts,), jnp.float32, low / len(shards), high / len(shards))
        factor_of = factor_of * jnp.repeat(jnp.exp(steps), dims[position] // parts).reshape((-1,) + (1,) * (len(dims) - 1 - position))
    return factor_of


def bell_draw(stream_key, extent, scale, limit, pieces=(), held_as=jnp.bfloat16):
    values = jax.random.normal(stream_key, extent, jnp.float32) * scale
    if len(pieces) > 0:
        values = shard_levels(stream_key, extent, pieces, -0.22, 0.18) * values
    return jnp.clip(values, min=-limit, max=limit).astype(held_as)


def setup_inputs(seed: int = 0) -> dict:
    keys = jax.random.split(jax.random.key(seed), 8)
    return {
        "vertical_profile_fields": bell_draw(keys[0], (VL, TOTAL_VERTICALS), 1.0, 6.0, ((1, 32),), jnp.float32),
        "implicit_diffusion_solver": bell_draw(keys[1], (VL, VL), VL ** -0.5, 0.4375, (), jnp.float32),
        "prior_seawater_warmth": bell_draw(keys[2], (TOTAL_VERTICALS,), 1.0, 6.0, ((0, 32),), jnp.float32),
        "overlay_share_matrices": jnp.clip(jnp.exp(math.log(0.015625) - 2.7725887 * jax.random.uniform(keys[3], (N_COMP * WTAB, BA, BO), jnp.float32) ** shard_levels(keys[3], (N_COMP * WTAB, BA, BO), ((0, 4),), -0.2, 0.2)), 0.0009765625, 0.015625),
        "overlay_pairings": draw_overlay_pairings(jax.random.fold_in(keys[7], 71), 0),
        "marine_top_fields": bell_draw(keys[5], (4, NOX, NOY), 1.0, 6.0, ((1, 4), (2, 8)), jnp.float32),
        "marine_indicator": plant((jax.random.randint(keys[6], (NOX, NOY), 0, 4) < 3).astype(jnp.int32), jax.random.fold_in(keys[6], 1), 0, 1),
    }


precise = lax.Precision.HIGHEST
wave_speed = 0.25
mixing = 0.15
rotation = 0.1
tracer_mixing = 0.2
forcing_rate = 0.05
transfer_constant = 0.5
dewpoint_moisture_limit = 0.6

def vertical_mixing_step(vertical_profile_fields, implicit_diffusion_solver, prior_seawater_warmth):
    renewed_profile_fields = jnp.dot(implicit_diffusion_solver, vertical_profile_fields, precision=precise, preferred_element_type=jnp.float32)
    lower_troposphere_warmth = renewed_profile_fields[VERTICAL_LAYERS - 1]
    moisture_content = renewed_profile_fields[2 * VERTICAL_LAYERS - 1]
    wind_east = renewed_profile_fields[3 * VERTICAL_LAYERS - 1]
    wind_north = renewed_profile_fields[4 * VERTICAL_LAYERS - 1]
    breeze_speed = jnp.sqrt(wind_east * wind_east + wind_north * wind_north + 1.0)
    conductive_energy_transfer = transfer_constant * breeze_speed * (prior_seawater_warmth - lower_troposphere_warmth)
    evaporation_rate = transfer_constant * breeze_speed * (dewpoint_moisture_limit * prior_seawater_warmth - moisture_content)
    stress_east = transfer_constant * breeze_speed * wind_east
    stress_north = transfer_constant * breeze_speed * wind_north
    return (renewed_profile_fields, jnp.stack([conductive_energy_transfer, evaporation_rate, stress_east, stress_north]))

def advance(padded, sea_mask, forcing):
    centre = padded[:, 1:-1, 1:-1]
    north_cells = padded[:, 2:, 1:-1]
    south_cells = padded[:, :-2, 1:-1]
    east_cells = padded[:, 1:-1, 2:]
    west_cells = padded[:, 1:-1, :-2]
    laplace = north_cells + south_cells + east_cells + west_cells - 4.0 * centre
    along_east = 0.5 * (east_cells - west_cells)
    along_north = 0.5 * (north_cells - south_cells)
    height = centre[0] - wave_speed * (along_east[1] + along_north[2]) + mixing * laplace[0] + forcing_rate * forcing[1]
    zonal_flow = centre[1] - wave_speed * along_east[0] + rotation * centre[2] + mixing * laplace[1] + forcing_rate * forcing[2]
    meridional_flow = centre[2] - wave_speed * along_north[0] - rotation * centre[1] + mixing * laplace[2] + forcing_rate * forcing[3]
    surface = centre[3] + tracer_mixing * laplace[3] + forcing_rate * forcing[0]
    return jnp.stack([height, zonal_flow, meridional_flow, surface]) * sea_mask

def reference(vertical_profile_fields, implicit_diffusion_solver, prior_seawater_warmth, overlay_share_matrices, overlay_pairings, marine_top_fields, marine_indicator):
    renewed_profile_fields, interface_transfers = vertical_mixing_step(vertical_profile_fields, implicit_diffusion_solver, prior_seawater_warmth)
    band_blocks = interface_transfers.reshape(F, N_COMP, N_TILE * ABLK, BA).transpose(1, 2, 0, 3)
    overlay_share_catalogue = overlay_share_matrices.reshape(N_COMP, WTAB, BA, BO)
    zonal_strip_members = overlay_pairings.reshape(3, N_COMP, N_TILE * OVL_DEV).transpose(1, 0, 2)

    def forward(inputs):
        blocks, weight_table, listing = inputs
        block_rows = listing[0] % N_TILE * ABLK + listing[0] // N_TILE
        combos = jnp.einsum('bfa,wao->bwfo', blocks, weight_table, precision=precise)
        contributions = combos[block_rows, listing[2]]
        return jnp.zeros((N_TILE * OX, F, BO), jnp.float32).at[listing[1]].add(contributions)
    forcing_bands = lax.map(forward, (band_blocks, overlay_share_catalogue, zonal_strip_members))
    forcing = forcing_bands.reshape(N_COMP, N_TILE, OX, F, BO).transpose(3, 0, 2, 1, 4).reshape(F, NOX, NOY)
    sea_mask = marine_indicator.astype(jnp.float32)

    def substep(substep_index, fields):
        return advance(jnp.pad(fields, ((0, 0), (1, 1), (1, 1))), sea_mask, forcing)
    marine_fields_stepped = lax.fori_loop(0, SUB, substep, marine_top_fields)
    meridional_strip_groups = marine_fields_stepped[3].reshape(N_COMP, OX, N_TILE, BO).transpose(0, 2, 1, 3).reshape(N_COMP, N_TILE * OX, BO)

    def backward_regrid(inputs):
        surface, weight_table, listing = inputs
        block_rows = listing[0] % N_TILE * ABLK + listing[0] // N_TILE
        picked = surface[listing[1]]
        combos = jnp.einsum('ko,wao->kwa', picked, weight_table, precision=precise)
        chosen = combos[jnp.arange(N_TILE * OVL_DEV), listing[2]]
        weight_sums = lax.optimization_barrier(jnp.sum(weight_table, axis=2))[listing[2]]
        numerator = jnp.zeros((N_TILE * ABLK, BA), jnp.float32).at[block_rows].add(chosen)
        denominator = jnp.zeros((N_TILE * ABLK, BA), jnp.float32).at[block_rows].add(weight_sums)
        return numerator / denominator
    seawater_warmth_regridded = lax.map(backward_regrid, (meridional_strip_groups, overlay_share_catalogue, zonal_strip_members)).reshape(TOTAL_VERTICALS)
    return (renewed_profile_fields, marine_fields_stepped, seawater_warmth_regridded)
```

```python
import functools
import jax
import jax.numpy as jnp
from jax import lax
from jax.experimental import pallas as pl
from jax.experimental.pallas import tpu as pltpu
from jax.sharding import PartitionSpec as P

VERTICAL_LAYERS = 48
F = 4
BA = 256
ABLK = 8
WTAB = 8
OX = 32
BO = 512
SUB = 20
HALO = 24
ROWS = OX + 2 * HALO
LANES = 128
WIDE = BO + LANES

wave_speed = 0.25
mixing = 0.15
rotation = 0.1
tracer_mixing = 0.2
forcing_rate = 0.05
transfer_constant = 0.5
dewpoint_moisture_limit = 0.6

MESH = pl.DeviceIdType.MESH
DIRECTIONS = [(dc, dt) for dc in (-1, 0, 1) for dt in (-1, 0, 1) if (dc, dt) != (0, 0)]
FIELDS_MASK = (0, 5)
FORCING = (5, 9)

NT = (((1,), (1,)), ((), ()))
NN = (((1,), (0,)), ((), ()))


def mm(a, b, dims):
    return lax.dot_general(a, b, dims, preferred_element_type=jnp.float32)


def split(x):
    high = x.astype(jnp.bfloat16)
    return high, (x - high.astype(jnp.float32)).astype(jnp.bfloat16)


def stencil_rows(x_ref, first, last):
    sub = lax.broadcasted_iota(jnp.int32, (8, WIDE), 0)
    top, bottom = sub == 0, sub == 7

    def tile(row):
        return [x_ref[f, row:row + 8, :] for f in range(4)]

    before = tile(max(first - 8, 0))
    here = tile(first)
    for row in range(first, last, 8):
        after = tile(row + 8) if row + 8 < ROWS else here
        north = [pltpu.roll(jnp.where(top, a, h), 7, 0) for a, h in zip(after, here)]
        south = [pltpu.roll(jnp.where(bottom, b, h), 1, 0) for b, h in zip(before, here)]
        east = [pltpu.roll(h, WIDE - 1, 1) for h in here]
        west = [pltpu.roll(h, 1, 1) for h in here]
        around = [(n + s) + (e + w) for n, s, e, w in zip(north, south, east, west)]
        mask = x_ref[4, row:row + 8, :]
        forced = [x_ref[5 + f, row:row + 8, :] for f in range(4)]
        half = 0.5 * wave_speed
        keep = 1.0 - 4.0 * mixing
        eta, u, v, t = here
        new = [
            keep * eta + mixing * around[0]
            - half * ((east[1] - west[1]) + (north[2] - south[2])) + forced[1],
            keep * u + mixing * around[1] - half * (east[0] - west[0])
            + rotation * v + forced[2],
            keep * v + mixing * around[2] - half * (north[0] - south[0])
            - rotation * u + forced[3],
            (1.0 - 4.0 * tracer_mixing) * t + tracer_mixing * around[3] + forced[0],
        ]
        for f in range(4):
            x_ref[f, row:row + 8, :] = new[f] * mask
        before, here = here, after


def kernel(nc, nt, flux_ref, list_ref, w_hbm, fields_ref, mask_ref, out_ref, sst_ref,
           flux_all, list_all, w_ref, w_hi, w_lo, x_ref, side_ref, counts, counts_t, lhs,
           z_ref, part_out, part_in, denom,
           w_sem, flux_send, flux_recv, list_send, list_recv, part_send, part_recv,
           halo_send, halo_recv):
    comp, tile = lax.axis_index("comp"), lax.axis_index("tile")
    w_copy = pltpu.make_async_copy(w_hbm, w_ref, w_sem)
    w_copy.start()

    def inside(dc, dt):
        ok = None
        for pos, step, size in ((comp, dc, nc), (tile, dt, nt)):
            here = None
            if step > 0:
                here = pos + step < size
            if step < 0:
                here = pos + step >= 0
            if here is not None:
                ok = here if ok is None else jnp.logical_and(ok, here)
        return ok

    x_ref[:, 0:HALO, :] = jnp.zeros((9, HALO, WIDE), jnp.float32)
    x_ref[:, HALO + OX:ROWS, :] = jnp.zeros((9, HALO, WIDE), jnp.float32)
    side_ref[...] = jnp.zeros_like(side_ref)
    x_ref[0:4, HALO:HALO + OX, 0:BO] = fields_ref[...]
    x_ref[4, HALO:HALO + OX, 0:BO] = mask_ref[...].astype(jnp.float32)
    flux_all[tile] = flux_ref[...]
    list_all[tile] = list_ref[...]

    barrier = pltpu.get_barrier_semaphore()

    def greet(d, carry):
        pl.semaphore_signal(
            barrier, inc=1, device_id=(comp, lax.rem(tile + d, nt)), device_id_type=MESH
        )
        return carry

    lax.fori_loop(1, nt, greet, 0)
    far = [d for d in DIRECTIONS if d[0] != 0]
    for dc, dt in far:
        @pl.when(inside(dc, dt))
        def _():
            pl.semaphore_signal(
                barrier, inc=1, device_id=(comp + dc, tile + dt), device_id_type=MESH
            )
    beside = [
        jnp.minimum(pos, 1) + jnp.minimum(size - 1 - pos, 1)
        for pos, size in ((comp, nc), (tile, nt))
    ]
    pl.semaphore_wait(barrier, nt - 1 + beside[0] * (1 + beside[1]))

    def peer_copy(src, dst, send, recv, d):
        return pltpu.make_async_remote_copy(
            src_ref=src, dst_ref=dst, send_sem=send.at[d], recv_sem=recv.at[d],
            device_id=(comp, lax.rem(tile + d, nt)), device_id_type=MESH,
        )

    def list_copy(d):
        return peer_copy(list_ref, list_all.at[tile], list_send, list_recv, d)

    def flux_copy(d):
        return peer_copy(flux_ref, flux_all.at[tile], flux_send, flux_recv, d)

    def part_copy(d):
        return peer_copy(
            part_out.at[lax.rem(tile + d, nt)], part_in.at[tile], part_send, part_recv, d
        )

    def each_peer(action):
        def step(d, carry):
            action(d)
            return carry
        lax.fori_loop(1, nt, step, 0)

    each_peer(lambda d: list_copy(d).start())
    each_peer(lambda d: flux_copy(d).start())

    def halo_copy(phase, number):
        dc, dt = DIRECTIONS[number]
        low, high = FIELDS_MASK if phase == 0 else FORCING
        planes = pl.ds(low, high - low)
        if dc == 0:
            src_rows, dst_rows = pl.ds(HALO, OX), pl.ds(HALO, OX)
        elif dc > 0:
            src_rows, dst_rows = pl.ds(OX, HALO), pl.ds(0, HALO)
        else:
            src_rows, dst_rows = pl.ds(HALO, HALO), pl.ds(HALO + OX, HALO)
        if dt == 0:
            src = x_ref.at[planes, src_rows, pl.ds(0, BO)]
            dst = x_ref.at[planes, dst_rows, pl.ds(0, BO)]
        elif dt > 0:
            src = x_ref.at[planes, src_rows, pl.ds(BO - LANES, LANES)]
            dst = side_ref.at[0, planes, dst_rows, :]
        else:
            src = x_ref.at[planes, src_rows, pl.ds(0, LANES)]
            dst = side_ref.at[1, planes, dst_rows, :]
        return pltpu.make_async_remote_copy(
            src_ref=src, dst_ref=dst,
            send_sem=halo_send.at[phase, number], recv_sem=halo_recv.at[phase, number],
            device_id=(comp + dc, tile + dt), device_id_type=MESH,
        )

    def halo_start(phase):
        for number, (dc, dt) in enumerate(DIRECTIONS):
            @pl.when(inside(dc, dt))
            def _():
                halo_copy(phase, number).start()

    def halo_wait(phase):
        for number, (dc, dt) in enumerate(DIRECTIONS):
            @pl.when(inside(dc, dt))
            def _():
                halo_copy(phase, number).wait_send()

            @pl.when(inside(-dc, -dt))
            def _():
                halo_copy(phase, number).wait_recv()

    halo_start(0)

    mine = list_ref[...]
    row8 = lax.broadcasted_iota(jnp.int32, (8, LANES), 0)
    own_block = (row8 == mine[0:1, :]).astype(jnp.bfloat16)
    own_weight = (row8 == mine[3:4, :]).astype(jnp.bfloat16)
    named = mm(own_block, own_weight, NT)
    ones = jnp.ones((16, BO), jnp.bfloat16)
    w_copy.wait()
    total = jnp.zeros((ABLK, BA), jnp.float32)
    for w in range(WTAB):
        high, low = split(w_ref[w])
        w_hi[w] = high
        w_lo[w] = low
        sums = mm(ones, high, NT) + mm(ones, low, NT)
        total = total + named[:, w:w + 1] * sums[0:ABLK, :]
    denom[...] = total

    each_peer(lambda d: list_copy(d).wait())
    counts[...] = jnp.zeros_like(counts)
    counts_t[...] = jnp.zeros_like(counts_t)

    def count(source, carry):
        listing = list_all[source]
        code = jnp.where(listing[1:2, :] == tile, listing[3:4, :] * OX + listing[2:3, :], -1)
        group = lax.broadcasted_iota(jnp.int32, (WTAB * OX, LANES), 0) == code
        block = lax.broadcasted_iota(jnp.int32, (nt * ABLK, LANES), 0) == (
            jnp.where(listing[0:1, :] >= 0, source * ABLK + listing[0:1, :], -1)
        )
        group, block = group.astype(jnp.bfloat16), block.astype(jnp.bfloat16)
        counts[...] += mm(group, block, NT)
        counts_t[...] += mm(block, group, NT)
        return carry

    lax.fori_loop(0, nt, count, 0)
    count_fw = counts[...].astype(jnp.bfloat16)

    each_peer(lambda d: flux_copy(d).wait())
    for f in range(F):
        high, low = split(flux_all[:, f].reshape(nt * ABLK, BA))
        grouped = mm(count_fw, high, NN) + mm(count_fw, low, NN)
        high, low = split(grouped)
        for w in range(WTAB):
            lhs[w, f * OX:(f + 1) * OX, :] = high[w * OX:(w + 1) * OX]
            lhs[w, (F + f) * OX:(F + f + 1) * OX, :] = low[w * OX:(w + 1) * OX]
    half = F * OX
    acc = jnp.zeros((half, BO), jnp.float32)
    for w in range(WTAB):
        both = mm(lhs[w], w_hi[w], NN)
        acc = acc + ((both[half:] + mm(lhs[w, 0:half, :], w_lo[w], NN)) + both[:half])
    acc = acc * forcing_rate
    for f in range(F):
        x_ref[5 + f, HALO:HALO + OX, 0:BO] = acc[f * OX:(f + 1) * OX]
    halo_start(1)
    halo_wait(0)
    halo_wait(1)

    lane = lax.broadcasted_iota(jnp.int32, (ROWS, LANES), 1)
    for k in range(9):
        x_ref[k, :, BO:WIDE] = jnp.where(lane < LANES // 2, side_ref[1, k], side_ref[0, k])

    done = 0
    while done < SUB:
        def window(step):
            depth = SUB - step
            return (HALO - depth) // 8 * 8, -(-(HALO + OX + depth) // 8) * 8
        first, last = window(done + 1)
        upto = done + 1
        while upto < SUB and window(upto + 1) == (first, last):
            upto += 1

        def substep(i, carry):
            stencil_rows(x_ref, first, last)
            return carry

        lax.fori_loop(0, upto - done, substep, 0)
        done = upto

    out_ref[...] = x_ref[0:4, HALO:HALO + OX, 0:BO]
    high, low = split(x_ref[3, HALO:HALO + OX, 0:BO])
    both = jnp.concatenate([high, low], axis=0)
    for w in range(WTAB):
        product = mm(both, w_hi[w], NT)
        z_ref[w * OX:(w + 1) * OX, :] = product[:OX] + (product[OX:] + mm(high, w_lo[w], NT))
    count_bw = counts_t[...].astype(jnp.bfloat16)
    high, low = split(z_ref[...])
    partial = mm(count_bw, high, NN) + mm(count_bw, low, NN)
    part_out[...] = partial.reshape(nt, ABLK, BA)
    each_peer(lambda d: part_copy(d).start())
    part_in[tile] = part_out[tile]
    each_peer(lambda d: part_copy(d).wait())
    sst_ref[...] = jnp.sum(part_in[...], axis=0) / denom[...]


def body(nc, nt, columns, solver, warmth, weights, pairings, fields, indicator):
    renewed = jnp.dot(
        solver, columns, precision=lax.Precision.HIGHEST, preferred_element_type=jnp.float32
    )
    air, moisture, wind_east, wind_north = (
        renewed[k * VERTICAL_LAYERS - 1] for k in (1, 2, 3, 4)
    )
    speed = transfer_constant * jnp.sqrt(wind_east * wind_east + wind_north * wind_north + 1.0)
    flux = jnp.stack([
        speed * (warmth - air),
        speed * (dewpoint_moisture_limit * warmth - moisture),
        speed * wind_east,
        speed * wind_north,
    ]).reshape(F, ABLK, BA)
    listing = jnp.stack([
        pairings[0] // nt, pairings[1] // OX, pairings[1] % OX, pairings[2]
    ])
    listing = jnp.pad(
        listing, ((0, 8 - 4), (0, LANES - listing.shape[1])), constant_values=-1
    )
    vmem = pl.BlockSpec(memory_space=pltpu.VMEM)
    f32, bf16 = jnp.float32, jnp.bfloat16
    dma = pltpu.SemaphoreType.DMA
    stepped, regridded = pl.pallas_call(
        functools.partial(kernel, nc, nt),
        out_shape=(
            jax.ShapeDtypeStruct((4, OX, BO), f32), jax.ShapeDtypeStruct((ABLK, BA), f32)
        ),
        in_specs=[vmem, vmem, pl.BlockSpec(memory_space=pl.ANY), vmem, vmem],
        out_specs=(vmem, vmem),
        scratch_shapes=[
            pltpu.VMEM((nt, F, ABLK, BA), f32),
            pltpu.VMEM((nt, 8, LANES), jnp.int32),
            pltpu.VMEM((WTAB, BA, BO), f32),
            pltpu.VMEM((WTAB, BA, BO), bf16),
            pltpu.VMEM((WTAB, BA, BO), bf16),
            pltpu.VMEM((9, ROWS, WIDE), f32),
            pltpu.VMEM((2, 9, ROWS, LANES), f32),
            pltpu.VMEM((WTAB * OX, nt * ABLK), f32),
            pltpu.VMEM((nt * ABLK, WTAB * OX), f32),
            pltpu.VMEM((WTAB, 2 * F * OX, BA), bf16),
            pltpu.VMEM((WTAB * OX, BA), f32),
            pltpu.VMEM((nt, ABLK, BA), f32),
            pltpu.VMEM((nt, ABLK, BA), f32),
            pltpu.VMEM((ABLK, BA), f32),
            dma,
            dma((nt,)), dma((nt,)), dma((nt,)), dma((nt,)), dma((nt,)), dma((nt,)),
            dma((2, 8)), dma((2, 8)),
        ],
        compiler_params=pltpu.CompilerParams(
            collective_id=0, has_side_effects=True, vmem_limit_bytes=48 * 1024 * 1024
        ),
        name="coupling",
    )(flux, listing, weights, fields, indicator)
    return renewed, stepped, regridded.reshape(-1)


def solution(mesh):
    placed = (
        P(None, ("comp", "tile")),
        P(),
        P(("comp", "tile")),
        P("comp", None, None),
        P(None, ("comp", "tile")),
        P(None, "comp", "tile"),
        P("comp", "tile"),
    )
    return jax.shard_map(
        functools.partial(body, mesh.shape["comp"], mesh.shape["tile"]),
        mesh=mesh,
        in_specs=placed,
        out_specs=(P(None, ("comp", "tile")), P(None, "comp", "tile"), P(("comp", "tile"))),
        check_vma=False,
    )
```

```python
import functools
import jax
import jax.numpy as jnp
from jax import lax
from jax.experimental import pallas as pl
from jax.experimental.pallas import tpu as pltpu
from jax.sharding import PartitionSpec as P

VERTICAL_LAYERS = 48
F = 4
BA = 256
ABLK = 8
WTAB = 8
OX = 32
BO = 512
SUB = 20
HALO = 24
ROWS = OX + 2 * HALO
LANES = 128
WIDE = BO + LANES

wave_speed = 0.25
mixing = 0.15
rotation = 0.1
tracer_mixing = 0.2
forcing_rate = 0.05
transfer_constant = 0.5
dewpoint_moisture_limit = 0.6

MESH = pl.DeviceIdType.MESH
DIRECTIONS = [(-1, 0), (1, 0), (-1, -1), (-1, 1), (1, -1), (1, 1), (0, -1), (0, 1)]
STRIP = 32
KINDS = [(0, 4), (4, 5), (5, 9)]

NT = (((1,), (1,)), ((), ()))
NN = (((1,), (0,)), ((), ()))


def mm(a, b, dims):
    return lax.dot_general(a, b, dims, preferred_element_type=jnp.float32)


def split(x):
    high = x.astype(jnp.bfloat16)
    return high, (x - high.astype(jnp.float32)).astype(jnp.bfloat16)


def stencil_rows(x_ref, first, last):
    sub = lax.broadcasted_iota(jnp.int32, (8, WIDE), 0)
    top, bottom = sub == 0, sub == 7

    def tile(row):
        return [x_ref[f, row:row + 8, :] for f in range(4)]

    before = tile(max(first - 8, 0))
    here = tile(first)
    for row in range(first, last, 8):
        after = tile(row + 8) if row + 8 < ROWS else here
        north = [pltpu.roll(jnp.where(top, a, h), 7, 0) for a, h in zip(after, here)]
        south = [pltpu.roll(jnp.where(bottom, b, h), 1, 0) for b, h in zip(before, here)]
        east = [pltpu.roll(h, WIDE - 1, 1) for h in here]
        west = [pltpu.roll(h, 1, 1) for h in here]
        around = [(n + s) + (e + w) for n, s, e, w in zip(north, south, east, west)]
        mask = x_ref[4, row:row + 8, :]
        forced = [x_ref[5 + f, row:row + 8, :] for f in range(4)]
        half = 0.5 * wave_speed
        keep = 1.0 - 4.0 * mixing
        eta, u, v, t = here
        new = [
            keep * eta + mixing * around[0]
            - half * ((east[1] - west[1]) + (north[2] - south[2])) + forced[1],
            keep * u + mixing * around[1] - half * (east[0] - west[0])
            + rotation * v + forced[2],
            keep * v + mixing * around[2] - half * (north[0] - south[0])
            - rotation * u + forced[3],
            (1.0 - 4.0 * tracer_mixing) * t + tracer_mixing * around[3] + forced[0],
        ]
        for f in range(4):
            x_ref[f, row:row + 8, :] = new[f] * mask
        before, here = here, after


def kernel(nc, nt, flux_ref, list_ref, w_hbm, fields_ref, mask_ref, out_ref, sst_ref,
           flux_all, list_all, w_ref, w_hi, w_lo, x_ref, side_ref, pack_ref, counts, counts_t, lhs,
           z_ref, part_out, part_in, denom,
           w_sem, flux_send, flux_recv, list_send, list_recv, part_send, part_recv,
           halo_send, halo_recv):
    comp, tile = lax.axis_index("comp"), lax.axis_index("tile")
    w_copy = pltpu.make_async_copy(w_hbm, w_ref, w_sem)
    w_copy.start()

    def inside(dc, dt):
        ok = None
        for pos, step, size in ((comp, dc, nc), (tile, dt, nt)):
            here = None
            if step > 0:
                here = pos + step < size
            if step < 0:
                here = pos + step >= 0
            if here is not None:
                ok = here if ok is None else jnp.logical_and(ok, here)
        return ok

    x_ref[:, 0:HALO, 0:BO] = jnp.zeros((9, HALO, BO), jnp.float32)
    x_ref[:, HALO + OX:ROWS, 0:BO] = jnp.zeros((9, HALO, BO), jnp.float32)
    side_ref[...] = jnp.zeros_like(side_ref)

    barrier = pltpu.get_barrier_semaphore()

    def greet(d, carry):
        pl.semaphore_signal(
            barrier, inc=1, device_id=(comp, lax.rem(tile + d, nt)), device_id_type=MESH
        )
        return carry

    lax.fori_loop(1, nt, greet, 0)
    far = [d for d in DIRECTIONS if d[0] != 0]
    for dc, dt in far:
        @pl.when(inside(dc, dt))
        def _():
            pl.semaphore_signal(
                barrier, inc=1, device_id=(comp + dc, tile + dt), device_id_type=MESH
            )
    own = pl.ds(HALO, OX)
    quarter = lax.broadcasted_iota(jnp.int32, (OX, LANES), 1) // STRIP

    def pack(kind):
        low, high = KINDS[kind]
        for side, column in ((0, BO - LANES), (1, 0)):
            packed = jnp.zeros((OX, LANES), jnp.float32)
            for f in range(high - low):
                strip = x_ref[low + f, own, column:column + LANES]
                shift = (STRIP * f + (STRIP if side == 0 else 0)) % LANES
                if shift:
                    strip = pltpu.roll(strip, shift, 1)
                packed = jnp.where(quarter == f, strip, packed)
            pack_ref[side, kind] = packed

    lane = lax.broadcasted_iota(jnp.int32, (ROWS, LANES), 1)

    def unpack(kind):
        low, high = KINDS[kind]
        for f in range(high - low):
            left, right = side_ref[0, kind], side_ref[1, kind]
            if f < 3:
                left = pltpu.roll(left, LANES - STRIP - STRIP * f, 1)
            if f > 0:
                right = pltpu.roll(right, LANES - STRIP * f, 1)
            x_ref[low + f, :, BO:WIDE] = jnp.where(
                lane < STRIP, right, jnp.where(lane >= LANES - STRIP, left, 0.0)
            )

    x_ref[0:4, own, 0:BO] = fields_ref[...]
    x_ref[4, own, 0:BO] = mask_ref[...].astype(jnp.float32)
    pack(0)
    pack(1)
    beside = [
        jnp.minimum(pos, 1) + jnp.minimum(size - 1 - pos, 1)
        for pos, size in ((comp, nc), (tile, nt))
    ]
    pl.semaphore_wait(barrier, nt - 1 + beside[0] * (1 + beside[1]))

    def peer_copy(src, dst, send, recv, d):
        return pltpu.make_async_remote_copy(
            src_ref=src, dst_ref=dst, send_sem=send.at[d], recv_sem=recv.at[d],
            device_id=(comp, lax.rem(tile + d, nt)), device_id_type=MESH,
        )

    def list_copy(d):
        return peer_copy(list_ref, list_all.at[tile], list_send, list_recv, d)

    def flux_copy(d):
        return peer_copy(flux_ref, flux_all.at[tile], flux_send, flux_recv, d)

    def part_copy(d):
        return peer_copy(
            part_out.at[lax.rem(tile + d, nt)], part_in.at[tile], part_send, part_recv, d
        )

    def each_peer(action):
        def step(d, carry):
            action(d)
            return carry
        lax.fori_loop(1, nt, step, 0)

    each_peer(lambda d: list_copy(d).start())
    each_peer(lambda d: flux_copy(d).start())

    def halo_copy(phase, number):
        dc, dt = DIRECTIONS[number]
        planes = pl.ds(0, 5) if phase == 0 else pl.ds(5, 4)
        kinds = pl.ds(0, 2) if phase == 0 else pl.ds(2, 1)
        if dc == 0:
            src_rows, dst_rows = pl.ds(HALO, OX), pl.ds(HALO, OX)
        elif dc > 0:
            src_rows, dst_rows = pl.ds(OX, HALO), pl.ds(0, HALO)
        else:
            src_rows, dst_rows = pl.ds(HALO, HALO), pl.ds(HALO + OX, HALO)
        if dt == 0:
            src = x_ref.at[planes, src_rows, pl.ds(0, BO)]
            dst = x_ref.at[planes, dst_rows, pl.ds(0, BO)]
        else:
            side = 0 if dt > 0 else 1
            pack_rows = {0: pl.ds(0, OX), 1: pl.ds(OX - HALO, HALO), -1: pl.ds(0, HALO)}[dc]
            src = pack_ref.at[side, kinds, pack_rows, :]
            dst = side_ref.at[side, kinds, dst_rows, :]
        return pltpu.make_async_remote_copy(
            src_ref=src, dst_ref=dst,
            send_sem=halo_send.at[phase, number], recv_sem=halo_recv.at[phase, number],
            device_id=(comp + dc, tile + dt), device_id_type=MESH,
        )

    def halo_start(phase):
        for number, (dc, dt) in enumerate(DIRECTIONS):
            @pl.when(inside(dc, dt))
            def _():
                halo_copy(phase, number).start()

    def halo_wait(phase):
        for number, (dc, dt) in enumerate(DIRECTIONS):
            @pl.when(inside(dc, dt))
            def _():
                halo_copy(phase, number).wait_send()

            @pl.when(inside(-dc, -dt))
            def _():
                halo_copy(phase, number).wait_recv()

    halo_start(0)
    flux_all[tile] = flux_ref[...]
    list_all[tile] = list_ref[...]

    mine = list_ref[...]
    row8 = lax.broadcasted_iota(jnp.int32, (8, LANES), 0)
    own_block = (row8 * nt + tile == mine[0:1, :]).astype(jnp.bfloat16)
    own_weight = (row8 == mine[2:3, :]).astype(jnp.bfloat16)
    named = mm(own_block, own_weight, NT)
    ones = jnp.ones((16, BO), jnp.bfloat16)
    w_copy.wait()
    total = jnp.zeros((ABLK, BA), jnp.float32)
    for w in range(WTAB):
        high, low = split(w_ref[w])
        w_hi[w] = high
        w_lo[w] = low
        sums = mm(ones, high, NT) + mm(ones, low, NT)
        total = total + named[:, w:w + 1] * sums[0:ABLK, :]
    denom[...] = total

    each_peer(lambda d: list_copy(d).wait())
    counts[...] = jnp.zeros_like(counts)
    counts_t[...] = jnp.zeros_like(counts_t)

    def count(source, carry):
        listing = list_all[source]
        row = listing[1:2, :] - tile * OX
        here = jnp.logical_and(row >= 0, row < OX)
        code = jnp.where(here, listing[2:3, :] * OX + row, -1)
        group = lax.broadcasted_iota(jnp.int32, (WTAB * OX, LANES), 0) == code
        number = lax.broadcasted_iota(jnp.int32, (nt * ABLK, LANES), 0) - source * ABLK
        number = jnp.where(jnp.logical_and(number >= 0, number < ABLK), number * nt + source, -2)
        block = number == listing[0:1, :]
        group, block = group.astype(jnp.bfloat16), block.astype(jnp.bfloat16)
        counts[...] += mm(group, block, NT)
        counts_t[...] += mm(block, group, NT)
        return carry

    lax.fori_loop(0, nt, count, 0)
    count_fw = counts[...].astype(jnp.bfloat16)

    each_peer(lambda d: flux_copy(d).wait())
    for f in range(F):
        high, low = split(flux_all[:, f].reshape(nt * ABLK, BA))
        grouped = mm(count_fw, high, NN) + mm(count_fw, low, NN)
        high, low = split(grouped)
        for w in range(WTAB):
            lhs[w, f * OX:(f + 1) * OX, :] = high[w * OX:(w + 1) * OX]
            lhs[w, (F + f) * OX:(F + f + 1) * OX, :] = low[w * OX:(w + 1) * OX]
    half = F * OX
    acc = jnp.zeros((half, BO), jnp.float32)
    for w in range(WTAB):
        both = mm(lhs[w], w_hi[w], NN)
        acc = acc + ((both[half:] + mm(lhs[w, 0:half, :], w_lo[w], NN)) + both[:half])
    acc = acc * forcing_rate
    for f in range(F):
        x_ref[5 + f, HALO:HALO + OX, 0:BO] = acc[f * OX:(f + 1) * OX]
    pack(2)
    halo_start(1)
    halo_wait(0)
    unpack(0)
    unpack(1)
    halo_wait(1)
    unpack(2)

    done = 0
    while done < SUB:
        def window(step):
            depth = SUB - step
            return (HALO - depth) // 8 * 8, -(-(HALO + OX + depth) // 8) * 8
        first, last = window(done + 1)
        upto = done + 1
        while upto < SUB and window(upto + 1) == (first, last):
            upto += 1

        def substep(i, carry):
            stencil_rows(x_ref, first, last)
            return carry

        lax.fori_loop(0, upto - done, substep, 0)
        done = upto

    out_ref[...] = x_ref[0:4, HALO:HALO + OX, 0:BO]
    high, low = split(x_ref[3, HALO:HALO + OX, 0:BO])
    both = jnp.concatenate([high, low], axis=0)
    for w in range(WTAB):
        product = mm(both, w_hi[w], NT)
        z_ref[w * OX:(w + 1) * OX, :] = product[:OX] + (product[OX:] + mm(high, w_lo[w], NT))
    count_bw = counts_t[...].astype(jnp.bfloat16)
    high, low = split(z_ref[...])
    partial = mm(count_bw, high, NN) + mm(count_bw, low, NN)
    part_out[...] = partial.reshape(nt, ABLK, BA)
    each_peer(lambda d: part_copy(d).start())
    part_in[tile] = part_out[tile]
    each_peer(lambda d: part_copy(d).wait())
    regridded = jnp.sum(part_in[...], axis=0) / denom[...]
    for k in range(BA // LANES):
        sst_ref[pl.ds(k, ABLK, stride=BA // LANES), :] = (
            regridded[:, k * LANES:(k + 1) * LANES]
        )


def body(nc, nt, columns, solver, warmth, weights, pairings, fields, indicator):
    renewed = jnp.dot(
        solver, columns, precision=lax.Precision.HIGH, preferred_element_type=jnp.float32
    )
    air, moisture, wind_east, wind_north = (
        renewed[k * VERTICAL_LAYERS - 1] for k in (1, 2, 3, 4)
    )
    speed = transfer_constant * jnp.sqrt(wind_east * wind_east + wind_north * wind_north + 1.0)
    flux = jnp.stack([
        speed * (warmth - air),
        speed * (dewpoint_moisture_limit * warmth - moisture),
        speed * wind_east,
        speed * wind_north,
    ]).reshape(F, ABLK, BA)
    listing = jnp.pad(
        pairings, ((0, 8 - 3), (0, LANES - pairings.shape[1])), constant_values=-1
    )
    vmem = pl.BlockSpec(memory_space=pltpu.VMEM)
    f32, bf16 = jnp.float32, jnp.bfloat16
    dma = pltpu.SemaphoreType.DMA
    stepped, regridded = pl.pallas_call(
        functools.partial(kernel, nc, nt),
        out_shape=(
            jax.ShapeDtypeStruct((4, OX, BO), f32), jax.ShapeDtypeStruct((ABLK * BA // LANES, LANES), f32)
        ),
        in_specs=[vmem, vmem, pl.BlockSpec(memory_space=pltpu.HBM), vmem, vmem],
        out_specs=(vmem, vmem),
        scratch_shapes=[
            pltpu.VMEM((nt, F, ABLK, BA), f32),
            pltpu.VMEM((nt, 8, LANES), jnp.int32),
            pltpu.VMEM((WTAB, BA, BO), f32),
            pltpu.VMEM((WTAB, BA, BO), bf16),
            pltpu.VMEM((WTAB, BA, BO), bf16),
            pltpu.VMEM((9, ROWS, WIDE), f32),
            pltpu.VMEM((2, 3, ROWS, LANES), f32),
            pltpu.VMEM((2, 3, OX, LANES), f32),
            pltpu.VMEM((WTAB * OX, nt * ABLK), f32),
            pltpu.VMEM((nt * ABLK, WTAB * OX), f32),
            pltpu.VMEM((WTAB, 2 * F * OX, BA), bf16),
            pltpu.VMEM((WTAB * OX, BA), f32),
            pltpu.VMEM((nt, ABLK, BA), f32),
            pltpu.VMEM((nt, ABLK, BA), f32),
            pltpu.VMEM((ABLK, BA), f32),
            dma,
            dma((nt,)), dma((nt,)), dma((nt,)), dma((nt,)), dma((nt,)), dma((nt,)),
            dma((2, 8)), dma((2, 8)),
        ],
        compiler_params=pltpu.CompilerParams(
            collective_id=0, has_side_effects=True, vmem_limit_bytes=60 * 1024 * 1024
        ),
        name="coupling",
    )(flux, listing, weights, fields, indicator)
    return renewed, stepped, regridded.reshape(-1)


def solution(mesh):
    placed = (
        P(None, ("comp", "tile")),
        P(),
        P(("comp", "tile")),
        P("comp", None, None),
        P(None, ("comp", "tile")),
        P(None, "comp", "tile"),
        P("comp", "tile"),
    )
    return jax.shard_map(
        functools.partial(body, mesh.shape["comp"], mesh.shape["tile"]),
        mesh=mesh,
        in_specs=placed,
        out_specs=(P(None, ("comp", "tile")), P(None, "comp", "tile"), P(("comp", "tile"))),
        check_vma=False,
    )
```

```python
import functools
import jax
import jax.numpy as jnp
from jax import lax
from jax.experimental import pallas as pl
from jax.experimental.pallas import tpu as pltpu
from jax.sharding import PartitionSpec as P

VERTICAL_LAYERS = 48
F = 4
BA = 256
ABLK = 8
WTAB = 8
OX = 32
BO = 512
SUB = 20
HALO = 24
ROWS = OX + 2 * HALO
LANES = 128
WIDE = BO + LANES

wave_speed = 0.25
mixing = 0.15
rotation = 0.1
tracer_mixing = 0.2
forcing_rate = 0.05
transfer_constant = 0.5
dewpoint_moisture_limit = 0.6

MESH = pl.DeviceIdType.MESH
DIRECTIONS = [(-1, 0), (1, 0), (-1, -1), (-1, 1), (1, -1), (1, 1), (0, -1), (0, 1)]
STRIP = 32
KINDS = [(0, 4), (4, 5), (5, 9)]

NT = (((1,), (1,)), ((), ()))
NN = (((1,), (0,)), ((), ()))


def mm(a, b, dims):
    return lax.dot_general(a, b, dims, preferred_element_type=jnp.float32)


def split(x):
    high = x.astype(jnp.bfloat16)
    return high, (x - high.astype(jnp.float32)).astype(jnp.bfloat16)


def stencil_rows(x_ref, first, last):
    sub = lax.broadcasted_iota(jnp.int32, (8, WIDE), 0)
    top, bottom = sub == 0, sub == 7

    def tile(row):
        return [x_ref[f, row:row + 8, :] for f in range(4)]

    before = tile(max(first - 8, 0))
    here = tile(first)
    for row in range(first, last, 8):
        after = tile(row + 8) if row + 8 < ROWS else here
        north = [pltpu.roll(jnp.where(top, a, h), 7, 0) for a, h in zip(after, here)]
        south = [pltpu.roll(jnp.where(bottom, b, h), 1, 0) for b, h in zip(before, here)]
        east = [pltpu.roll(h, WIDE - 1, 1) for h in here]
        west = [pltpu.roll(h, 1, 1) for h in here]
        around = [(n + s) + (e + w) for n, s, e, w in zip(north, south, east, west)]
        mask = x_ref[4, row:row + 8, :]
        forced = [x_ref[5 + f, row:row + 8, :] for f in range(4)]
        half = 0.5 * wave_speed
        keep = 1.0 - 4.0 * mixing
        eta, u, v, t = here
        new = [
            keep * eta + mixing * around[0]
            - half * ((east[1] - west[1]) + (north[2] - south[2])) + forced[1],
            keep * u + mixing * around[1] - half * (east[0] - west[0])
            + rotation * v + forced[2],
            keep * v + mixing * around[2] - half * (north[0] - south[0])
            - rotation * u + forced[3],
            (1.0 - 4.0 * tracer_mixing) * t + tracer_mixing * around[3] + forced[0],
        ]
        for f in range(4):
            x_ref[f, row:row + 8, :] = new[f] * mask
        before, here = here, after


def kernel(nc, nt, columns_hbm, solver_ref, warmth_ref, pairs_ref, w_hbm, fields_ref, mask_ref,
           out_ref, sst_ref, columns_ref, products, flux_ref, list_ref, columns_sem, flux_all, list_all, w_ref, w_hi, w_lo, x_ref, side_ref, pack_ref, counts, counts_t, lhs,
           z_ref, part_out, part_in, denom,
           w_sem, flux_send, flux_recv, list_send, list_recv, part_send, part_recv,
           halo_send, halo_recv):
    comp, tile = lax.axis_index("comp"), lax.axis_index("tile")
    w_copy = pltpu.make_async_copy(w_hbm, w_ref, w_sem)
    w_copy.start()
    columns_copy = pltpu.make_async_copy(columns_hbm, columns_ref, columns_sem)
    columns_copy.start()

    def inside(dc, dt):
        ok = None
        for pos, step, size in ((comp, dc, nc), (tile, dt, nt)):
            here = None
            if step > 0:
                here = pos + step < size
            if step < 0:
                here = pos + step >= 0
            if here is not None:
                ok = here if ok is None else jnp.logical_and(ok, here)
        return ok

    x_ref[:, 0:HALO, 0:BO] = jnp.zeros((9, HALO, BO), jnp.float32)
    x_ref[:, HALO + OX:ROWS, 0:BO] = jnp.zeros((9, HALO, BO), jnp.float32)
    side_ref[...] = jnp.zeros_like(side_ref)

    barrier = pltpu.get_barrier_semaphore()

    def greet(d, carry):
        pl.semaphore_signal(
            barrier, inc=1, device_id=(comp, lax.rem(tile + d, nt)), device_id_type=MESH
        )
        return carry

    lax.fori_loop(1, nt, greet, 0)
    far = [d for d in DIRECTIONS if d[0] != 0]
    for dc, dt in far:
        @pl.when(inside(dc, dt))
        def _():
            pl.semaphore_signal(
                barrier, inc=1, device_id=(comp + dc, tile + dt), device_id_type=MESH
            )
    own = pl.ds(HALO, OX)
    quarter = lax.broadcasted_iota(jnp.int32, (OX, LANES), 1) // STRIP

    def pack(kind):
        low, high = KINDS[kind]
        for side, column in ((0, BO - LANES), (1, 0)):
            packed = jnp.zeros((OX, LANES), jnp.float32)
            for f in range(high - low):
                strip = x_ref[low + f, own, column:column + LANES]
                shift = (STRIP * f + (STRIP if side == 0 else 0)) % LANES
                if shift:
                    strip = pltpu.roll(strip, shift, 1)
                packed = jnp.where(quarter == f, strip, packed)
            pack_ref[side, kind] = packed

    lane = lax.broadcasted_iota(jnp.int32, (ROWS, LANES), 1)

    def unpack(kind):
        low, high = KINDS[kind]
        for f in range(high - low):
            left, right = side_ref[0, kind], side_ref[1, kind]
            if f < 3:
                left = pltpu.roll(left, LANES - STRIP - STRIP * f, 1)
            if f > 0:
                right = pltpu.roll(right, LANES - STRIP * f, 1)
            x_ref[low + f, :, BO:WIDE] = jnp.where(
                lane < STRIP, right, jnp.where(lane >= LANES - STRIP, left, 0.0)
            )

    list_ref[...] = jnp.full((8, LANES), -1, jnp.int32)
    list_ref[0:3, 0:pairs_ref.shape[1]] = pairs_ref[...]
    x_ref[0:4, own, 0:BO] = fields_ref[...]
    x_ref[4, own, 0:BO] = mask_ref[...].astype(jnp.float32)
    pack(0)
    pack(1)
    beside = [
        jnp.minimum(pos, 1) + jnp.minimum(size - 1 - pos, 1)
        for pos, size in ((comp, nc), (tile, nt))
    ]
    pl.semaphore_wait(barrier, nt - 1 + beside[0] * (1 + beside[1]))

    def peer_copy(src, dst, send, recv, d):
        return pltpu.make_async_remote_copy(
            src_ref=src, dst_ref=dst, send_sem=send.at[d], recv_sem=recv.at[d],
            device_id=(comp, lax.rem(tile + d, nt)), device_id_type=MESH,
        )

    def list_copy(d):
        return peer_copy(list_ref, list_all.at[tile], list_send, list_recv, d)

    def flux_copy(d):
        return peer_copy(flux_ref, flux_all.at[tile], flux_send, flux_recv, d)

    def part_copy(d):
        return peer_copy(
            part_out.at[lax.rem(tile + d, nt)], part_in.at[tile], part_send, part_recv, d
        )

    def each_peer(action):
        def step(d, carry):
            action(d)
            return carry
        lax.fori_loop(1, nt, step, 0)

    each_peer(lambda d: list_copy(d).start())

    def halo_copy(phase, number):
        dc, dt = DIRECTIONS[number]
        planes = pl.ds(0, 5) if phase == 0 else pl.ds(5, 4)
        kinds = pl.ds(0, 2) if phase == 0 else pl.ds(2, 1)
        if dc == 0:
            src_rows, dst_rows = pl.ds(HALO, OX), pl.ds(HALO, OX)
        elif dc > 0:
            src_rows, dst_rows = pl.ds(OX, HALO), pl.ds(0, HALO)
        else:
            src_rows, dst_rows = pl.ds(HALO, HALO), pl.ds(HALO + OX, HALO)
        if dt == 0:
            src = x_ref.at[planes, src_rows, pl.ds(0, BO)]
            dst = x_ref.at[planes, dst_rows, pl.ds(0, BO)]
        else:
            side = 0 if dt > 0 else 1
            pack_rows = {0: pl.ds(0, OX), 1: pl.ds(OX - HALO, HALO), -1: pl.ds(0, HALO)}[dc]
            src = pack_ref.at[side, kinds, pack_rows, :]
            dst = side_ref.at[side, kinds, dst_rows, :]
        return pltpu.make_async_remote_copy(
            src_ref=src, dst_ref=dst,
            send_sem=halo_send.at[phase, number], recv_sem=halo_recv.at[phase, number],
            device_id=(comp + dc, tile + dt), device_id_type=MESH,
        )

    def halo_start(phase):
        for number, (dc, dt) in enumerate(DIRECTIONS):
            @pl.when(inside(dc, dt))
            def _():
                halo_copy(phase, number).start()

    def halo_wait(phase):
        for number, (dc, dt) in enumerate(DIRECTIONS):
            @pl.when(inside(dc, dt))
            def _():
                halo_copy(phase, number).wait_send()

            @pl.when(inside(-dc, -dt))
            def _():
                halo_copy(phase, number).wait_recv()

    halo_start(0)

    rows = jnp.concatenate(
        [solver_ref[k * VERTICAL_LAYERS - 1:k * VERTICAL_LAYERS, :] for k in range(1, 5)], axis=0
    )
    rest = rows - rows.astype(jnp.bfloat16).astype(jnp.float32)
    rows = jnp.concatenate([rows, rest, jnp.zeros((8, rows.shape[1]), jnp.float32)], axis=0)
    rows = rows.astype(jnp.bfloat16)
    columns_copy.wait()
    high, low = split(columns_ref[...])
    first, second = mm(rows, high, NN), mm(rows, low, NN)
    mixed = first[0:4] + (first[4:8] + second[0:4])
    for f in range(F):
        for j in range(ABLK):
            products[f, j:j + 1, :] = mixed[f:f + 1, j * BA:(j + 1) * BA]
    pieces = BA // LANES
    warmth = jnp.concatenate(
        [warmth_ref[pl.ds(k, ABLK, stride=pieces), :] for k in range(pieces)], axis=1
    )
    air, moisture, wind_east, wind_north = (products[f] for f in range(F))
    speed = transfer_constant * jnp.sqrt(wind_east * wind_east + wind_north * wind_north + 1.0)
    flux_ref[0] = speed * (warmth - air)
    flux_ref[1] = speed * (dewpoint_moisture_limit * warmth - moisture)
    flux_ref[2] = speed * wind_east
    flux_ref[3] = speed * wind_north
    each_peer(lambda d: flux_copy(d).start())
    flux_all[tile] = flux_ref[...]
    list_all[tile] = list_ref[...]

    mine = list_ref[...]
    row8 = lax.broadcasted_iota(jnp.int32, (8, LANES), 0)
    own_block = (row8 * nt + tile == mine[0:1, :]).astype(jnp.bfloat16)
    own_weight = (row8 == mine[2:3, :]).astype(jnp.bfloat16)
    named = mm(own_block, own_weight, NT)
    ones = jnp.ones((16, BO), jnp.bfloat16)
    w_copy.wait()
    total = jnp.zeros((ABLK, BA), jnp.float32)
    for w in range(WTAB):
        high, low = split(w_ref[w])
        w_hi[w] = high
        w_lo[w] = low
        sums = mm(ones, high, NT) + mm(ones, low, NT)
        total = total + named[:, w:w + 1] * sums[0:ABLK, :]
    denom[...] = total

    each_peer(lambda d: list_copy(d).wait())
    counts[...] = jnp.zeros_like(counts)
    counts_t[...] = jnp.zeros_like(counts_t)

    def count(source, carry):
        listing = list_all[source]
        row = listing[1:2, :] - tile * OX
        here = jnp.logical_and(row >= 0, row < OX)
        code = jnp.where(here, listing[2:3, :] * OX + row, -1)
        group = lax.broadcasted_iota(jnp.int32, (WTAB * OX, LANES), 0) == code
        number = lax.broadcasted_iota(jnp.int32, (nt * ABLK, LANES), 0) - source * ABLK
        number = jnp.where(jnp.logical_and(number >= 0, number < ABLK), number * nt + source, -2)
        block = number == listing[0:1, :]
        group, block = group.astype(jnp.bfloat16), block.astype(jnp.bfloat16)
        counts[...] += mm(group, block, NT)
        counts_t[...] += mm(block, group, NT)
        return carry

    lax.fori_loop(0, nt, count, 0)
    count_fw = counts[...].astype(jnp.bfloat16)

    each_peer(lambda d: flux_copy(d).wait())
    for f in range(F):
        high, low = split(flux_all[:, f].reshape(nt * ABLK, BA))
        grouped = mm(count_fw, high, NN) + mm(count_fw, low, NN)
        high, low = split(grouped)
        for w in range(WTAB):
            lhs[w, f * OX:(f + 1) * OX, :] = high[w * OX:(w + 1) * OX]
            lhs[w, (F + f) * OX:(F + f + 1) * OX, :] = low[w * OX:(w + 1) * OX]
    half = F * OX
    acc = jnp.zeros((half, BO), jnp.float32)
    for w in range(WTAB):
        both = mm(lhs[w], w_hi[w], NN)
        acc = acc + ((both[half:] + mm(lhs[w, 0:half, :], w_lo[w], NN)) + both[:half])
    acc = acc * forcing_rate
    for f in range(F):
        x_ref[5 + f, HALO:HALO + OX, 0:BO] = acc[f * OX:(f + 1) * OX]
    pack(2)
    halo_start(1)
    halo_wait(0)
    unpack(0)
    unpack(1)
    halo_wait(1)
    unpack(2)

    done = 0
    while done < SUB:
        def window(step):
            depth = SUB - step
            return (HALO - depth) // 8 * 8, -(-(HALO + OX + depth) // 8) * 8
        first, last = window(done + 1)
        upto = done + 1
        while upto < SUB and window(upto + 1) == (first, last):
            upto += 1

        def substep(i, carry):
            stencil_rows(x_ref, first, last)
            return carry

        lax.fori_loop(0, upto - done, substep, 0)
        done = upto

    out_ref[...] = x_ref[0:4, HALO:HALO + OX, 0:BO]
    high, low = split(x_ref[3, HALO:HALO + OX, 0:BO])
    both = jnp.concatenate([high, low], axis=0)
    for w in range(WTAB):
        product = mm(both, w_hi[w], NT)
        z_ref[w * OX:(w + 1) * OX, :] = product[:OX] + (product[OX:] + mm(high, w_lo[w], NT))
    count_bw = counts_t[...].astype(jnp.bfloat16)
    high, low = split(z_ref[...])
    partial = mm(count_bw, high, NN) + mm(count_bw, low, NN)
    part_out[...] = partial.reshape(nt, ABLK, BA)
    each_peer(lambda d: part_copy(d).start())
    part_in[tile] = part_out[tile]
    each_peer(lambda d: part_copy(d).wait())
    regridded = jnp.sum(part_in[...], axis=0) / denom[...]
    for k in range(BA // LANES):
        sst_ref[pl.ds(k, ABLK, stride=BA // LANES), :] = (
            regridded[:, k * LANES:(k + 1) * LANES]
        )


def body(nc, nt, columns, solver, warmth, weights, pairings, fields, indicator):
    renewed = jnp.dot(
        solver, columns, precision=lax.Precision.HIGH, preferred_element_type=jnp.float32
    )
    vmem = pl.BlockSpec(memory_space=pltpu.VMEM)
    hbm = pl.BlockSpec(memory_space=pltpu.HBM)
    f32, bf16 = jnp.float32, jnp.bfloat16
    dma = pltpu.SemaphoreType.DMA
    stepped, regridded = pl.pallas_call(
        functools.partial(kernel, nc, nt),
        out_shape=(
            jax.ShapeDtypeStruct((4, OX, BO), f32), jax.ShapeDtypeStruct((ABLK * BA // LANES, LANES), f32)
        ),
        in_specs=[hbm, vmem, vmem, vmem, hbm, vmem, vmem],
        out_specs=(vmem, vmem),
        scratch_shapes=[
            pltpu.VMEM(columns.shape, f32),
            pltpu.VMEM((F, ABLK, BA), f32),
            pltpu.VMEM((F, ABLK, BA), f32),
            pltpu.VMEM((8, LANES), jnp.int32),
            dma,
            pltpu.VMEM((nt, F, ABLK, BA), f32),
            pltpu.VMEM((nt, 8, LANES), jnp.int32),
            pltpu.VMEM((WTAB, BA, BO), f32),
            pltpu.VMEM((WTAB, BA, BO), bf16),
            pltpu.VMEM((WTAB, BA, BO), bf16),
            pltpu.VMEM((9, ROWS, WIDE), f32),
            pltpu.VMEM((2, 3, ROWS, LANES), f32),
            pltpu.VMEM((2, 3, OX, LANES), f32),
            pltpu.VMEM((WTAB * OX, nt * ABLK), f32),
            pltpu.VMEM((nt * ABLK, WTAB * OX), f32),
            pltpu.VMEM((WTAB, 2 * F * OX, BA), bf16),
            pltpu.VMEM((WTAB * OX, BA), f32),
            pltpu.VMEM((nt, ABLK, BA), f32),
            pltpu.VMEM((nt, ABLK, BA), f32),
            pltpu.VMEM((ABLK, BA), f32),
            dma,
            dma((nt,)), dma((nt,)), dma((nt,)), dma((nt,)), dma((nt,)), dma((nt,)),
            dma((2, 8)), dma((2, 8)),
        ],
        compiler_params=pltpu.CompilerParams(
            collective_id=0, has_side_effects=True, vmem_limit_bytes=60 * 1024 * 1024
        ),
        name="coupling",
    )(columns, solver, warmth.reshape(-1, LANES), pairings, weights, fields, indicator)
    return renewed, stepped, regridded.reshape(-1)


def solution(mesh):
    placed = (
        P(None, ("comp", "tile")),
        P(),
        P(("comp", "tile")),
        P("comp", None, None),
        P(None, ("comp", "tile")),
        P(None, "comp", "tile"),
        P("comp", "tile"),
    )
    return jax.shard_map(
        functools.partial(body, mesh.shape["comp"], mesh.shape["tile"]),
        mesh=mesh,
        in_specs=placed,
        out_specs=(P(None, ("comp", "tile")), P(None, "comp", "tile"), P(("comp", "tile"))),
        check_vma=False,
    )
```

```python
import functools
import jax
import jax.numpy as jnp
from jax import lax
from jax.experimental import pallas as pl
from jax.experimental.pallas import tpu as pltpu
from jax.sharding import PartitionSpec as P

VERTICAL_LAYERS = 48
F = 4
BA = 256
ABLK = 8
WTAB = 8
OX = 32
BO = 512
SUB = 20
HALO = 24
ROWS = OX + 2 * HALO
LANES = 128
WIDE = BO + LANES

wave_speed = 0.25
mixing = 0.15
rotation = 0.1
tracer_mixing = 0.2
forcing_rate = 0.05
transfer_constant = 0.5
dewpoint_moisture_limit = 0.6

MESH = pl.DeviceIdType.MESH
DIRECTIONS = [(-1, 0), (1, 0), (-1, -1), (-1, 1), (1, -1), (1, 1), (0, -1), (0, 1)]
STRIP = 32
KINDS = [(0, 4), (4, 5), (5, 9)]

NT = (((1,), (1,)), ((), ()))
NN = (((1,), (0,)), ((), ()))


def mm(a, b, dims):
    return lax.dot_general(a, b, dims, preferred_element_type=jnp.float32)


def split(x):
    high = x.astype(jnp.bfloat16)
    return high, (x - high.astype(jnp.float32)).astype(jnp.bfloat16)


def stencil_rows(x_ref, first, last):
    sub = lax.broadcasted_iota(jnp.int32, (8, WIDE), 0)
    top, bottom = sub == 0, sub == 7

    def tile(row):
        return [x_ref[f, row:row + 8, :] for f in range(4)]

    before = tile(max(first - 8, 0))
    here = tile(first)
    for row in range(first, last, 8):
        after = tile(row + 8) if row + 8 < ROWS else here
        north = [pltpu.roll(jnp.where(top, a, h), 7, 0) for a, h in zip(after, here)]
        south = [pltpu.roll(jnp.where(bottom, b, h), 1, 0) for b, h in zip(before, here)]
        east = [pltpu.roll(h, WIDE - 1, 1) for h in here]
        west = [pltpu.roll(h, 1, 1) for h in here]
        around = [(n + s) + (e + w) for n, s, e, w in zip(north, south, east, west)]
        mask = x_ref[4, row:row + 8, :]
        forced = [x_ref[5 + f, row:row + 8, :] for f in range(4)]
        half = 0.5 * wave_speed
        keep = 1.0 - 4.0 * mixing
        eta, u, v, t = here
        new = [
            keep * eta + mixing * around[0]
            - half * ((east[1] - west[1]) + (north[2] - south[2])) + forced[1],
            keep * u + mixing * around[1] - half * (east[0] - west[0])
            + rotation * v + forced[2],
            keep * v + mixing * around[2] - half * (north[0] - south[0])
            - rotation * u + forced[3],
            (1.0 - 4.0 * tracer_mixing) * t + tracer_mixing * around[3] + forced[0],
        ]
        for f in range(4):
            x_ref[f, row:row + 8, :] = new[f] * mask
        before, here = here, after


def kernel(nc, nt, columns_hbm, solver_ref, warmth_ref, pairs_ref, w_hbm, fields_ref, mask_ref,
           out_ref, sst_ref, columns_ref, products, flux_ref, list_ref, columns_sem, flux_all, list_all, w_ref, w_hi, w_lo, x_ref, side_ref, pack_ref, counts, counts_t, lhs,
           z_ref, part_out, part_in, denom,
           w_sem, flux_send, flux_recv, list_send, list_recv, part_send, part_recv,
           halo_send, halo_recv):
    comp, tile = lax.axis_index("comp"), lax.axis_index("tile")
    w_copy = pltpu.make_async_copy(w_hbm, w_ref, w_sem)
    w_copy.start()
    columns_copy = pltpu.make_async_copy(columns_hbm, columns_ref, columns_sem)
    columns_copy.start()

    def inside(dc, dt):
        ok = None
        for pos, step, size in ((comp, dc, nc), (tile, dt, nt)):
            here = None
            if step > 0:
                here = pos + step < size
            if step < 0:
                here = pos + step >= 0
            if here is not None:
                ok = here if ok is None else jnp.logical_and(ok, here)
        return ok

    x_ref[:, 0:HALO, 0:BO] = jnp.zeros((9, HALO, BO), jnp.float32)
    x_ref[:, HALO + OX:ROWS, 0:BO] = jnp.zeros((9, HALO, BO), jnp.float32)
    side_ref[...] = jnp.zeros_like(side_ref)

    barrier = pltpu.get_barrier_semaphore()

    def greet(d, carry):
        pl.semaphore_signal(
            barrier, inc=1, device_id=(comp, lax.rem(tile + d, nt)), device_id_type=MESH
        )
        return carry

    lax.fori_loop(1, nt, greet, 0)
    far = [d for d in DIRECTIONS if d[0] != 0]
    for dc, dt in far:
        @pl.when(inside(dc, dt))
        def _():
            pl.semaphore_signal(
                barrier, inc=1, device_id=(comp + dc, tile + dt), device_id_type=MESH
            )
    own = pl.ds(HALO, OX)
    quarter = lax.broadcasted_iota(jnp.int32, (OX, LANES), 1) // STRIP

    def pack(kind):
        low, high = KINDS[kind]
        for side, column in ((0, BO - LANES), (1, 0)):
            packed = jnp.zeros((OX, LANES), jnp.float32)
            for f in range(high - low):
                strip = x_ref[low + f, own, column:column + LANES]
                shift = (STRIP * f + (STRIP if side == 0 else 0)) % LANES
                if shift:
                    strip = pltpu.roll(strip, shift, 1)
                packed = jnp.where(quarter == f, strip, packed)
            pack_ref[side, kind] = packed

    lane = lax.broadcasted_iota(jnp.int32, (ROWS, LANES), 1)

    def unpack(kind):
        low, high = KINDS[kind]
        for f in range(high - low):
            left, right = side_ref[0, kind], side_ref[1, kind]
            if f < 3:
                left = pltpu.roll(left, LANES - STRIP - STRIP * f, 1)
            if f > 0:
                right = pltpu.roll(right, LANES - STRIP * f, 1)
            x_ref[low + f, :, BO:WIDE] = jnp.where(
                lane < STRIP, right, jnp.where(lane >= LANES - STRIP, left, 0.0)
            )

    list_ref[...] = jnp.full((8, LANES), -1, jnp.int32)
    list_ref[0:3, 0:pairs_ref.shape[1]] = pairs_ref[...]
    x_ref[0:4, own, 0:BO] = fields_ref[...]
    x_ref[4, own, 0:BO] = mask_ref[...].astype(jnp.float32)
    pack(0)
    pack(1)
    beside = [
        jnp.minimum(pos, 1) + jnp.minimum(size - 1 - pos, 1)
        for pos, size in ((comp, nc), (tile, nt))
    ]
    pl.semaphore_wait(barrier, nt - 1 + beside[0] * (1 + beside[1]))

    def peer_copy(src, dst, send, recv, d):
        return pltpu.make_async_remote_copy(
            src_ref=src, dst_ref=dst, send_sem=send.at[d], recv_sem=recv.at[d],
            device_id=(comp, lax.rem(tile + d, nt)), device_id_type=MESH,
        )

    def list_copy(d):
        return peer_copy(list_ref, list_all.at[tile], list_send, list_recv, d)

    def flux_copy(d):
        return peer_copy(flux_ref, flux_all.at[tile], flux_send, flux_recv, d)

    def part_copy(d):
        return peer_copy(
            part_out.at[lax.rem(tile + d, nt)], part_in.at[tile], part_send, part_recv, d
        )

    def each_peer(action):
        def step(d, carry):
            action(d)
            return carry
        lax.fori_loop(1, nt, step, 0)

    each_peer(lambda d: list_copy(d).start())

    def halo_copy(phase, number):
        dc, dt = DIRECTIONS[number]
        planes = pl.ds(0, 5) if phase == 0 else pl.ds(5, 4)
        kinds = pl.ds(0, 2) if phase == 0 else pl.ds(2, 1)
        if dc == 0:
            src_rows, dst_rows = pl.ds(HALO, OX), pl.ds(HALO, OX)
        elif dc > 0:
            src_rows, dst_rows = pl.ds(OX, HALO), pl.ds(0, HALO)
        else:
            src_rows, dst_rows = pl.ds(HALO, HALO), pl.ds(HALO + OX, HALO)
        if dt == 0:
            src = x_ref.at[planes, src_rows, pl.ds(0, BO)]
            dst = x_ref.at[planes, dst_rows, pl.ds(0, BO)]
        else:
            side = 0 if dt > 0 else 1
            pack_rows = {0: pl.ds(0, OX), 1: pl.ds(OX - HALO, HALO), -1: pl.ds(0, HALO)}[dc]
            src = pack_ref.at[side, kinds, pack_rows, :]
            dst = side_ref.at[side, kinds, dst_rows, :]
        return pltpu.make_async_remote_copy(
            src_ref=src, dst_ref=dst,
            send_sem=halo_send.at[phase, number], recv_sem=halo_recv.at[phase, number],
            device_id=(comp + dc, tile + dt), device_id_type=MESH,
        )

    def halo_start(phase, numbers=range(8)):
        for number in numbers:
            dc, dt = DIRECTIONS[number]

            @pl.when(inside(dc, dt))
            def _():
                halo_copy(phase, number).start()

    def halo_wait(phase):
        for number, (dc, dt) in enumerate(DIRECTIONS):
            @pl.when(inside(dc, dt))
            def _():
                halo_copy(phase, number).wait_send()

            @pl.when(inside(-dc, -dt))
            def _():
                halo_copy(phase, number).wait_recv()

    halo_start(0)

    rows = jnp.concatenate(
        [solver_ref[k * VERTICAL_LAYERS - 1:k * VERTICAL_LAYERS, :] for k in range(1, 5)], axis=0
    )
    rest = rows - rows.astype(jnp.bfloat16).astype(jnp.float32)
    rows = jnp.concatenate([rows, rest, jnp.zeros((8, rows.shape[1]), jnp.float32)], axis=0)
    rows = rows.astype(jnp.bfloat16)
    columns_copy.wait()
    high, low = split(columns_ref[...])
    first, second = mm(rows, high, NN), mm(rows, low, NN)
    mixed = first[0:4] + (first[4:8] + second[0:4])
    for f in range(F):
        for j in range(ABLK):
            products[f, j:j + 1, :] = mixed[f:f + 1, j * BA:(j + 1) * BA]
    pieces = BA // LANES
    warmth = jnp.concatenate(
        [warmth_ref[pl.ds(k, ABLK, stride=pieces), :] for k in range(pieces)], axis=1
    )
    air, moisture, wind_east, wind_north = (products[f] for f in range(F))
    speed = transfer_constant * jnp.sqrt(wind_east * wind_east + wind_north * wind_north + 1.0)
    flux_ref[0] = speed * (warmth - air)
    flux_ref[1] = speed * (dewpoint_moisture_limit * warmth - moisture)
    flux_ref[2] = speed * wind_east
    flux_ref[3] = speed * wind_north
    each_peer(lambda d: flux_copy(d).start())
    flux_all[tile] = flux_ref[...]
    list_all[tile] = list_ref[...]

    mine = list_ref[...]
    row8 = lax.broadcasted_iota(jnp.int32, (8, LANES), 0)
    own_block = (row8 * nt + tile == mine[0:1, :]).astype(jnp.bfloat16)
    own_weight = (row8 == mine[2:3, :]).astype(jnp.bfloat16)
    named = mm(own_block, own_weight, NT)
    ones = jnp.ones((16, BO), jnp.bfloat16)
    w_copy.wait()
    total = jnp.zeros((ABLK, BA), jnp.float32)
    for w in range(WTAB):
        high, low = split(w_ref[w])
        w_hi[w] = high
        w_lo[w] = low
        sums = mm(ones, high, NT) + mm(ones, low, NT)
        total = total + named[:, w:w + 1] * sums[0:ABLK, :]
    denom[...] = total

    each_peer(lambda d: list_copy(d).wait())
    counts[...] = jnp.zeros_like(counts)
    counts_t[...] = jnp.zeros_like(counts_t)

    def count(source, carry):
        listing = list_all[source]
        row = listing[1:2, :] - tile * OX
        here = jnp.logical_and(row >= 0, row < OX)
        code = jnp.where(here, listing[2:3, :] * OX + row, -1)
        group = lax.broadcasted_iota(jnp.int32, (WTAB * OX, LANES), 0) == code
        number = lax.broadcasted_iota(jnp.int32, (nt * ABLK, LANES), 0) - source * ABLK
        number = jnp.where(jnp.logical_and(number >= 0, number < ABLK), number * nt + source, -2)
        block = number == listing[0:1, :]
        group, block = group.astype(jnp.bfloat16), block.astype(jnp.bfloat16)
        counts[...] += mm(group, block, NT)
        counts_t[...] += mm(block, group, NT)
        return carry

    lax.fori_loop(0, nt, count, 0)
    count_fw = counts[...].astype(jnp.bfloat16)

    each_peer(lambda d: flux_copy(d).wait())
    for f in range(F):
        high, low = split(flux_all[:, f].reshape(nt * ABLK, BA))
        grouped = mm(count_fw, high, NN) + mm(count_fw, low, NN)
        high, low = split(grouped)
        for w in range(WTAB):
            lhs[w, f * OX:(f + 1) * OX, :] = high[w * OX:(w + 1) * OX]
            lhs[w, (F + f) * OX:(F + f + 1) * OX, :] = low[w * OX:(w + 1) * OX]
    half = F * OX
    acc = jnp.zeros((half, BO), jnp.float32)
    for w in range(WTAB):
        both = mm(lhs[w], w_hi[w], NN)
        acc = acc + ((both[half:] + mm(lhs[w, 0:half, :], w_lo[w], NN)) + both[:half])
    acc = acc * forcing_rate
    for f in range(F):
        x_ref[5 + f, HALO:HALO + OX, 0:BO] = acc[f * OX:(f + 1) * OX]
    halo_start(1, range(2))
    pack(2)
    halo_start(1, range(2, 8))
    halo_wait(0)
    unpack(0)
    unpack(1)
    halo_wait(1)
    unpack(2)

    done = 0
    while done < SUB:
        def window(step):
            depth = SUB - step
            return (HALO - depth) // 8 * 8, -(-(HALO + OX + depth) // 8) * 8
        first, last = window(done + 1)
        upto = done + 1
        while upto < SUB and window(upto + 1) == (first, last):
            upto += 1

        def substep(i, carry):
            stencil_rows(x_ref, first, last)
            return carry

        lax.fori_loop(0, upto - done, substep, 0)
        done = upto

    high, low = split(x_ref[3, HALO:HALO + OX, 0:BO])
    both = jnp.concatenate([high, low], axis=0)
    for w in range(WTAB):
        product = mm(both, w_hi[w], NT)
        z_ref[w * OX:(w + 1) * OX, :] = product[:OX] + (product[OX:] + mm(high, w_lo[w], NT))
    count_bw = counts_t[...].astype(jnp.bfloat16)
    high, low = split(z_ref[...])
    partial = mm(count_bw, high, NN) + mm(count_bw, low, NN)
    part_out[...] = partial.reshape(nt, ABLK, BA)
    each_peer(lambda d: part_copy(d).start())
    out_ref[...] = x_ref[0:4, HALO:HALO + OX, 0:BO]
    part_in[tile] = part_out[tile]
    each_peer(lambda d: part_copy(d).wait())
    regridded = jnp.sum(part_in[...], axis=0) / denom[...]
    for k in range(BA // LANES):
        sst_ref[pl.ds(k, ABLK, stride=BA // LANES), :] = (
            regridded[:, k * LANES:(k + 1) * LANES]
        )


def body(nc, nt, columns, solver, warmth, weights, pairings, fields, indicator):
    renewed = jnp.dot(
        solver, columns, precision=lax.Precision.HIGH, preferred_element_type=jnp.float32
    )
    vmem = pl.BlockSpec(memory_space=pltpu.VMEM)
    hbm = pl.BlockSpec(memory_space=pltpu.HBM)
    f32, bf16 = jnp.float32, jnp.bfloat16
    dma = pltpu.SemaphoreType.DMA
    stepped, regridded = pl.pallas_call(
        functools.partial(kernel, nc, nt),
        out_shape=(
            jax.ShapeDtypeStruct((4, OX, BO), f32), jax.ShapeDtypeStruct((ABLK * BA // LANES, LANES), f32)
        ),
        in_specs=[hbm, vmem, vmem, vmem, hbm, vmem, vmem],
        out_specs=(vmem, vmem),
        scratch_shapes=[
            pltpu.VMEM(columns.shape, f32),
            pltpu.VMEM((F, ABLK, BA), f32),
            pltpu.VMEM((F, ABLK, BA), f32),
            pltpu.VMEM((8, LANES), jnp.int32),
            dma,
            pltpu.VMEM((nt, F, ABLK, BA), f32),
            pltpu.VMEM((nt, 8, LANES), jnp.int32),
            pltpu.VMEM((WTAB, BA, BO), f32),
            pltpu.VMEM((WTAB, BA, BO), bf16),
            pltpu.VMEM((WTAB, BA, BO), bf16),
            pltpu.VMEM((9, ROWS, WIDE), f32),
            pltpu.VMEM((2, 3, ROWS, LANES), f32),
            pltpu.VMEM((2, 3, OX, LANES), f32),
            pltpu.VMEM((WTAB * OX, nt * ABLK), f32),
            pltpu.VMEM((nt * ABLK, WTAB * OX), f32),
            pltpu.VMEM((WTAB, 2 * F * OX, BA), bf16),
            pltpu.VMEM((WTAB * OX, BA), f32),
            pltpu.VMEM((nt, ABLK, BA), f32),
            pltpu.VMEM((nt, ABLK, BA), f32),
            pltpu.VMEM((ABLK, BA), f32),
            dma,
            dma((nt,)), dma((nt,)), dma((nt,)), dma((nt,)), dma((nt,)), dma((nt,)),
            dma((2, 8)), dma((2, 8)),
        ],
        compiler_params=pltpu.CompilerParams(
            collective_id=0, has_side_effects=True, vmem_limit_bytes=60 * 1024 * 1024
        ),
        name="coupling",
    )(columns, solver, warmth.reshape(-1, LANES), pairings, weights, fields, indicator)
    return renewed, stepped, regridded.reshape(-1)


def solution(mesh):
    placed = (
        P(None, ("comp", "tile")),
        P(),
        P(("comp", "tile")),
        P("comp", None, None),
        P(None, ("comp", "tile")),
        P(None, "comp", "tile"),
        P("comp", "tile"),
    )
    return jax.shard_map(
        functools.partial(body, mesh.shape["comp"], mesh.shape["tile"]),
        mesh=mesh,
        in_specs=placed,
        out_specs=(P(None, ("comp", "tile")), P(None, "comp", "tile"), P(("comp", "tile"))),
        check_vma=False,
    )
```
